128 devices in a mesh: row: 16 (over x, y), col: 8 (over z, core).
Axes of the slice: x: 4, y: 4, z: 4, core: 2. Of those that a mesh axis runs over, the one named last changes fastest.
Arguments:
- panel: bfloat16 [49152, 256], P('row', 'col'), as said below
- trailing: bfloat16 [49152, 16384], P('row', 'col'), may hold values from -6 to 6
- tile_list: int32 [352], P('row'), may hold values from 0 to 23, as said below
Outputs:
- triangle: float32 [256, 256], replicated
- top_rows: float32 [16384, 256], P('col')
- updated: bfloat16 [45056, 16384], P('row', 'col')
The draws below stay inside these ranges and needn't reach their ends.
Inputs may be any that keep to these rules, and one draw needn't show every extreme that they name: `tile_list`: each aligned block of 22 entries (the entries of one index of row) lists distinct tile numbers of that group's 24 tiles in increasing order and always includes tile 24 - 1. `panel`: the active rows of every row group, and all active rows together, have full column rank with a condition number under 100.
All inputs are finite; a program needn't handle non-finite values.
Results may differ from the reference program's by a relative error of at most 0.0065.
Values may be sent and summed in bfloat16 or wider, within the bound.
A program may use at most 128 MiB of HBM per device.

```python
import math
import jax
import jax.numpy as jnp
from jax import lax

TILE = 128
PANEL = 256
TRAIL = 16384
TILES_DEV = 24
ACTIVE_DEV = 22
ROWS = 49152
ACT_ALL = 352


def draw_panel(key, part):
    group_rows = TILES_DEV * TILE
    nblocks = ROWS // group_rows
    key_one, key_two = jax.random.split(jax.random.fold_in(key, 11), 2)
    exponent = jax.random.uniform(key_one, (ROWS, 1), jnp.float32)
    row_scale = jnp.exp(exponent * math.log(10.0))
    device_row = (jnp.arange(ROWS) // group_rows).astype(jnp.float32)
    fraction = device_row / max(nblocks - 1, 1)
    rising = jnp.sqrt(1.0 + 2.0 * fraction)
    base_draw = jax.random.normal(key_two, (ROWS, PANEL), jnp.float32)
    values = base_draw * row_scale * rising[:, None] / (4.0 * math.sqrt(ACT_ALL * TILE))
    return values.astype(jnp.bfloat16)


def draw_tile_list(key, part):
    nblocks = ACT_ALL // ACTIVE_DEV
    key_list = jax.random.split(jax.random.fold_in(key, 23), nblocks)

    def one_block(block_key):
        picked = jax.random.permutation(block_key, TILES_DEV - 1)[:ACTIVE_DEV - 1].astype(jnp.int32)
        joined = jnp.concatenate([picked, jnp.full((1,), TILES_DEV - 1, jnp.int32)])
        return jnp.sort(joined).astype(jnp.int32)
    return jax.vmap(one_block)(key_list).reshape(-1).astype(jnp.int32)


def with_spikes(array, key, source, target, parts, factor):
    owner, partner = [(jnp.arange(array.shape[position]) // (array.shape[position] // parts)).reshape([-1 if axis == position else 1 for axis in range(array.ndim)]) for position in (source, target)]
    chosen = jax.random.permutation(key, parts)[partner]
    strong = (owner == chosen) | (owner == (partner + parts // 2) % parts)
    return jnp.where(strong, factor * array, array)


def levels(key, dims, cuts, smallest, top_value):
    gain, own = 1.0, jax.random.fold_in(key, 6)
    for dim, shards_of in cuts:
        steps = jnp.exp(jax.random.uniform(jax.random.fold_in(own, dim), (shards_of,), jnp.float32, smallest / len(cuts), top_value / len(cuts)))
        gain = gain * jnp.repeat(steps, dims[dim] // shards_of).reshape([-1 if axis == dim else 1 for axis in range(len(dims))])
    return gain


def gaussian_with(stream_key, dims, deviation, reach, shards, heavy, kind=jnp.bfloat16):
    drawn = deviation * jax.random.normal(stream_key, dims, jnp.float32)
    if shards:
        drawn = drawn * levels(stream_key, dims, shards, -0.22, 0.18)
    return jnp.clip(with_spikes(drawn, jax.random.fold_in(stream_key, 3), *heavy), -reach, reach).astype(kind)


def setup_inputs(seed: int = 0) -> dict:
    splits = jax.random.split(jax.random.key(seed), 4)
    panel = draw_panel(jax.random.fold_in(splits[3], 71), 0)
    trailing = gaussian_with(splits[1], (ROWS, TRAIL), 1.0, 6.0, ((0, 16), (1, 8)), (0, 1, 16, 2.0))
    tile_list = draw_tile_list(jax.random.fold_in(splits[3], 71), 0)
    return dict(panel=panel, trailing=trailing, tile_list=tile_list)


def select_rows(whole, tile_list):
    nblocks = tile_list.shape[0] // ACTIVE_DEV
    offsets = (jnp.arange(nblocks, dtype=jnp.int32) * TILES_DEV)[:, None]
    tile_index = (tile_list.reshape(nblocks, ACTIVE_DEV).astype(jnp.int32) + offsets).reshape(-1).astype(jnp.int32)
    tiled = whole.reshape(-1, TILE, whole.shape[1])
    return jnp.take(tiled, tile_index, axis=0).reshape(-1, whole.shape[1])

def reference(panel, trailing, tile_list):
    act_panel = select_rows(panel, tile_list)
    act_trail = select_rows(trailing, tile_list)
    gram_matrix = lax.dot_general(act_panel.astype(jnp.float32), act_panel.astype(jnp.float32), (((0,), (0,)), ((), ())), preferred_element_type=jnp.float32)
    lower_factor = jnp.linalg.cholesky(gram_matrix)
    triangle = lower_factor.T
    cross_sum = lax.dot_general(act_trail.astype(jnp.float32), act_panel.astype(jnp.float32), (((0,), (0,)), ((), ())), preferred_element_type=jnp.float32)
    top_rows = jax.scipy.linalg.solve_triangular(lower_factor, cross_sum.T, lower=True).T
    coeff = jax.scipy.linalg.solve_triangular(lower_factor, top_rows.T, lower=True, trans=1).T.astype(jnp.bfloat16)
    product = lax.dot_general(act_panel.astype(jnp.float32), coeff.astype(jnp.float32), (((1,), (1,)), ((), ())), preferred_element_type=jnp.float32)
    updated = (act_trail.astype(jnp.float32) - product).astype(jnp.bfloat16)
    return (triangle, top_rows, updated)
```

```python
import functools

import jax
import jax.numpy as jnp
from jax import lax
from jax.experimental import pallas as pl
from jax.experimental.pallas import tpu as pltpu
from jax.sharding import PartitionSpec as P

TILE = 128
MESH = pl.DeviceIdType.MESH
F32 = jnp.float32
BF16 = jnp.bfloat16
HIGH = lax.Precision.HIGHEST


def dot(a, b, dims, precision=None):
    return lax.dot_general(a, b, (dims, ((), ())), precision=precision, preferred_element_type=F32)


def factor(a_ref, u_ref, m_ref, n, block):
    for k in range(n // block):
        lo = k * block
        slab = a_ref[lo : lo + block, :]
        rows = lax.broadcasted_iota(jnp.int32, (block, 1), 0)
        for j in range(block):
            scale = lax.rsqrt(slab[j : j + 1, lo + j : lo + j + 1])
            row = slab[j : j + 1, :] * scale
            col = slab[:, lo + j : lo + j + 1] * scale
            col = jnp.where(rows > j, col, 0.0)
            slab = jnp.where(rows == j, row, slab - col * row)
        u = slab[:, :n]
        cols = lax.broadcasted_iota(jnp.int32, (block, n), 1)
        keep = cols >= lax.broadcasted_iota(jnp.int32, (block, n), 0) + lo
        u_ref[lo : lo + block, :] = jnp.where(keep, u, 0.0)
        m_ref[lo : lo + block, :] = slab[:, n:]
        if lo + block < n:
            a_ref[lo + block :, :] -= dot(slab[:, lo + block : n], slab, ((0,), (0,)), HIGH)


def fetch_and_reduce(
    tl_ref, pt_ref, t_hbm,
    t_out, pt_out, cr_out, u_out, m_out,
    wide, gx, gy, gc, aug, s1, l1, s2, l2, agb,
    t_sem, p_send, p_recv, g_send, g_recv, c_send, c_recv,
):
    width, active = pt_ref.shape[0], tl_ref.shape[0]
    n = 8 * width
    tiles = t_out.shape[0]
    spare = tiles - active
    r, c = lax.axis_index("row"), lax.axis_index("col")
    x, y, z, k = r // 4, lax.rem(r, 4), c // 2, lax.rem(c, 2)

    def along_x(d):
        return (lax.rem(x + d, 4) * 4 + y, c)

    def along_y(d):
        return (x * 4 + lax.rem(y + d, 4), c)

    def along_z(d):
        return (r, lax.rem(z + d, 4) * 2 + k)

    sibling = (r, z * 2 + 1 - k)

    loads = []
    for i in range(6):
        copy = pltpu.make_async_copy(t_hbm.at[pl.ds(4 * i, 4)], t_out.at[pl.ds(4 * i, 4)], t_sem.at[i])
        copy.start()
        loads.append(copy)

    barrier = pltpu.get_barrier_semaphore()
    partners = [f(d) for f in (along_x, along_y, along_z) for d in (1, 2, 3)] + [sibling]
    for partner in partners:
        pl.semaphore_signal(barrier, inc=1, device_id=partner, device_id_type=MESH)

    for j in range(active):
        pick = pt_ref[:, (j + spare) * TILE : (j + spare + 1) * TILE]
        for i in reversed(range(spare)):
            pick = jnp.where(tl_ref[j] == j + i, pt_ref[:, (j + i) * TILE : (j + i + 1) * TILE], pick)
        pt_out[c, :, j * TILE : (j + 1) * TILE] = pick
    pl.semaphore_wait(barrier, len(partners))

    def send(src, dst, send_sem, recv_sem, to):
        copy = pltpu.make_async_remote_copy(
            src_ref=src, dst_ref=dst, send_sem=send_sem, recv_sem=recv_sem, device_id=to, device_id_type=MESH
        )
        copy.start()
        return copy

    def gather_col(ref, sends, recvs, base):
        mine = ref.at[c]
        out = [send(mine, mine, sends.at[base], recvs.at[base], sibling)]
        direct = {}
        for i, d in enumerate((1, 3, 2)):
            direct[d] = send(mine, mine, sends.at[base + 1 + i], recvs.at[base + 1 + i], along_z(d))
        return out, direct

    def relay_col(ref, sends, recvs, base, started):
        out, direct = started
        for i, d in enumerate((1, 3, 2)):
            direct[d].wait_recv()
            owner = ref.at[lax.rem(z + 4 - d, 4) * 2 + k]
            out.append(send(owner, owner, sends.at[base + 4 + i], recvs.at[base + 4 + i], sibling))
        for copy in out:
            copy.wait()
        for d in (1, 3, 2):
            direct[d].wait_send()

    started = gather_col(pt_out, p_send, p_recv, 0)
    relay_col(pt_out, p_send, p_recv, 0, started)

    pt_all = pt_out[...].reshape(n, active * TILE)
    gx[x] = dot(pt_out[c], pt_all, ((1,), (1,)))
    for j in range(tiles):
        spread = jnp.zeros((8, width, TILE), BF16)
        for i in range(max(j - spare, 0), min(j, active - 1) + 1):
            spread = jnp.where(tl_ref[i] == j, pt_out[:, :, i * TILE : (i + 1) * TILE], spread)
        wide[:, j * TILE : (j + 1) * TILE] = spread.reshape(n, TILE)
    g1 = [send(gx.at[x], gx.at[x], g_send.at[d - 1], g_recv.at[d - 1], along_x(d)) for d in (1, 2, 3)]

    for copy in loads:
        copy.wait()

    def first(q):
        return (along_x, along_y, x, y) if q % 2 == 0 else (along_y, along_x, y, x)

    def cross(q):
        for half in range(2):
            cols = slice(q * 512 + half * 256, q * 512 + half * 256 + 256)
            part = dot(wide[...], t_out[:, :, cols].reshape(tiles * TILE, 256), ((1,), (0,)))
            s1[q, 2 * half] = part[:, :128].astype(BF16)
            s1[q, 2 * half + 1] = part[:, 128:].astype(BF16)
        a, _, ma, _ = first(q)
        sent = []
        for d in (1, 2, 3):
            sem = 12 * q + d - 1
            sent.append(send(s1.at[q, lax.rem(ma + d, 4)], l1.at[q, d - 1], c_send.at[sem], c_recv.at[sem], a(d)))
        return sent

    stage1 = [cross(0)]
    for copy in g1:
        copy.wait()
    gy[y] = gx[0] + gx[1] + gx[2] + gx[3]
    g2 = [send(gy.at[y], gy.at[y], g_send.at[2 + d], g_recv.at[2 + d], along_y(d)) for d in (1, 2, 3)]
    stage1.append(cross(1))
    for copy in g2:
        copy.wait()
    gc[c] = gy[0] + gy[1] + gy[2] + gy[3]
    g3 = gather_col(gc, g_send, g_recv, 6)
    stage1.append(cross(2))
    stage1.append(cross(3))

    stage2 = []
    for q in range(4):
        _, b, ma, mb = first(q)
        for copy in stage1[q]:
            copy.wait()
        total = s1[q, ma].astype(F32)
        for d in range(3):
            total = total + l1[q, d].astype(F32)
        s2[q] = total.astype(BF16).reshape(4, n // 4, 128)
        sent = []
        for d in (1, 2, 3):
            sem = 12 * q + 2 + d
            sent.append(send(s2.at[q, lax.rem(mb + d, 4)], l2.at[q, d - 1], c_send.at[sem], c_recv.at[sem], b(d)))
        stage2.append(sent)
    stage3 = []
    for q in range(4):
        _, b, ma, mb = first(q)
        for copy in stage2[q]:
            copy.wait()
        total = s2[q, mb].astype(F32)
        for d in range(3):
            total = total + l2[q, d].astype(F32)
        agb[q, mb] = total.astype(BF16)
        sent = []
        for d in (1, 2, 3):
            sem = 12 * q + 5 + d
            sent.append(send(agb.at[q, mb], agb.at[q, mb], c_send.at[sem], c_recv.at[sem], b(d)))
        stage3.append(sent)
    relay_col(gc, g_send, g_recv, 6, g3)
    stage4 = []
    for q in range(4):
        a, _, ma, _ = first(q)
        for copy in stage3[q]:
            copy.wait()
        cr_out[q, ma] = agb[q].reshape(n, 128)
        sent = []
        for d in (1, 2, 3):
            sem = 12 * q + 8 + d
            sent.append(send(cr_out.at[q, ma], cr_out.at[q, ma], c_send.at[sem], c_recv.at[sem], a(d)))
        stage4.append(sent)

    aug[:, :n] = gc[...].reshape(n, n)
    eye = lax.broadcasted_iota(jnp.int32, (n, n), 0) == lax.broadcasted_iota(jnp.int32, (n, n), 1)
    aug[:, n:] = jnp.where(eye, 1.0, 0.0)
    factor(aug, u_out, m_out, n, 32)
    for sent in stage4:
        for copy in sent:
            copy.wait()


def finish(tl_ref, t_ref, pt_ref, cr_ref, u_ref, m_ref, tri_ref, top_hbm, up_hbm, coeff, tops, outs, top_sem, out_sem):
    n = m_ref.shape[0]
    active = tl_ref.shape[0]
    tri_ref[...] = u_ref[...]
    m = m_ref[...]
    mh = m.astype(BF16)
    ml = (m - mh.astype(F32)).astype(BF16)
    copies = []
    for q in range(4):
        part = jnp.concatenate([cr_ref[q, a] for a in range(4)], axis=1)
        top = dot(mh, part, ((1,), (0,))) + dot(ml, part, ((1,), (0,)))
        tops[q] = top.T
        copy = pltpu.make_async_copy(tops.at[q], top_hbm.at[pl.ds(q * 512, 512)], top_sem.at[q])
        copy.start()
        copies.append(copy)
        tb = top.astype(BF16)
        coeff[:, q * 512 : (q + 1) * 512] = (dot(mh, tb, ((0,), (0,))) + dot(ml, tb, ((0,), (0,)))).astype(BF16)
    pending = [None] * 3
    for i in range(active // 2):
        slot = i % 3
        if pending[slot] is not None:
            pending[slot].wait()
        cols = pt_ref[:, :, i * 256 : (i + 1) * 256].reshape(n, 256)
        product = dot(cols, coeff[...], ((0,), (0,)))
        outs[slot, :128] = (t_ref[tl_ref[2 * i]].astype(F32) - product[:128]).astype(BF16)
        outs[slot, 128:] = (t_ref[tl_ref[2 * i + 1]].astype(F32) - product[128:]).astype(BF16)
        copy = pltpu.make_async_copy(outs.at[slot], up_hbm.at[pl.ds(i * 256, 256)], out_sem.at[slot])
        copy.start()
        pending[slot] = copy
    for copy in pending + copies:
        copy.wait()


def local(panel, trailing, tile_list):
    rows, width = panel.shape
    cols = trailing.shape[1]
    active = tile_list.shape[0]
    tiles = rows // TILE
    n = 8 * width
    vmem = pl.BlockSpec(memory_space=pltpu.VMEM)
    smem = pl.BlockSpec(memory_space=pltpu.SMEM)
    anywhere = pl.BlockSpec(memory_space=pl.ANY)
    hbm = pl.BlockSpec(memory_space=pltpu.HBM)
    dma = pltpu.SemaphoreType.DMA
    t, pt, cr, u, m = pl.pallas_call(
        fetch_and_reduce,
        out_shape=(
            pltpu.VMEM((tiles, TILE, cols), BF16),
            pltpu.VMEM((8, width, active * TILE), BF16),
            pltpu.VMEM((4, 4, n, 128), BF16),
            pltpu.VMEM((n, n), F32),
            pltpu.VMEM((n, n), F32),
        ),
        in_specs=[smem, vmem, hbm],
        out_specs=[vmem] * 5,
        scratch_shapes=[
            pltpu.VMEM((n, rows), BF16),
            pltpu.VMEM((4, width, n), F32),
            pltpu.VMEM((4, width, n), F32),
            pltpu.VMEM((8, width, n), F32),
            pltpu.VMEM((n, 2 * n), F32),
            pltpu.VMEM((4, 4, n, 128), BF16),
            pltpu.VMEM((4, 3, n, 128), BF16),
            pltpu.VMEM((4, 4, n // 4, 128), BF16),
            pltpu.VMEM((4, 3, n // 4, 128), BF16),
            pltpu.VMEM((4, 4, n // 4, 128), BF16),
            dma((6,)),
            dma((7,)),
            dma((7,)),
            dma((13,)),
            dma((13,)),
            dma((48,)),
            dma((48,)),
        ],
        compiler_params=pltpu.CompilerParams(collective_id=0, has_side_effects=True, vmem_limit_bytes=24 * 2**20),
    )(tile_list, panel.T, trailing.reshape(tiles, TILE, cols))
    return pl.pallas_call(
        finish,
        out_shape=(
            jax.ShapeDtypeStruct((n, n), F32),
            jax.ShapeDtypeStruct((cols, n), F32),
            jax.ShapeDtypeStruct((active * TILE, cols), BF16),
        ),
        in_specs=[smem] + [vmem] * 5,
        out_specs=[vmem, anywhere, anywhere],
        scratch_shapes=[
            pltpu.VMEM((n, cols), BF16),
            pltpu.VMEM((4, cols // 4, n), F32),
            pltpu.VMEM((3, 2 * TILE, cols), BF16),
            dma((4,)),
            dma((3,)),
        ],
        compiler_params=pltpu.CompilerParams(vmem_limit_bytes=24 * 2**20),
    )(tile_list, t, pt, cr, u, m)


def solution(mesh):
    return jax.shard_map(
        local,
        mesh=mesh,
        in_specs=(P("row", "col"), P("row", "col"), P("row")),
        out_specs=(P(), P("col", None), P("row", "col")),
        check_vma=False,
    )
```

```python
import functools

import jax
import jax.numpy as jnp
from jax import lax
from jax.experimental import pallas as pl
from jax.experimental.pallas import tpu as pltpu
from jax.sharding import PartitionSpec as P

TILE = 128
MESH = pl.DeviceIdType.MESH
F32 = jnp.float32
BF16 = jnp.bfloat16
HIGH = lax.Precision.HIGHEST


def dot(a, b, dims, precision=None):
    return lax.dot_general(a, b, (dims, ((), ())), precision=precision, preferred_element_type=F32)


def spread_entries(d, p):
    a, low, inv = {}, {}, {}
    for i in range(p):
        for j in range(i + 1):
            a[i, j] = jnp.broadcast_to(d[j : j + 1, i : i + 1], (8, 128))
    for j in range(p):
        inv[j, j] = lax.rsqrt(a[j, j])
        for i in range(j, p):
            low[i, j] = a[i, j] * inv[j, j]
        for k in range(j + 1, p):
            for i in range(k, p):
                a[i, k] = a[i, k] - low[i, j] * low[k, j]
    for i in range(p):
        for j in range(i):
            total = sum(low[i, k] * inv[k, j] for k in range(j, i))
            inv[i, j] = -total * inv[i, i]
    return inv


def factor(a_ref, u_ref, m_ref, n, block, p=8):
    wide = 2 * n // 128
    rows = lax.broadcasted_iota(jnp.int32, (8, 128), 0)

    def across(column):
        return jnp.concatenate([column] * wide, axis=1)

    for lo in range(0, n, block):
        groups = [a_ref[lo + i : lo + i + p, :] for i in range(0, block, p)]
        done = []
        for g in range(block // p):
            at = lo + g * p
            inv = spread_entries(groups[g][:, at : at + p], p)
            u = None
            for j in range(p):
                column = jnp.zeros((8, 128), F32)
                for i in range(j, p):
                    column = jnp.where(rows == i, inv[i, j], column)
                term = across(column) * groups[g][j : j + 1, :]
                u = term if u is None else u + term
            done.append(u)
            for h in range(g + 1, block // p):
                left = [jnp.broadcast_to(groups[h][:, at + q : at + q + 1], (8, 128)) for q in range(p)]
                rest = groups[h]
                for j in range(p):
                    column = sum(left[q] * inv[j, q] for q in range(j + 1))
                    rest = rest - across(column) * u[j : j + 1, :]
                groups[h] = rest
            yield
        full = jnp.concatenate(done, axis=0)
        keep = lax.broadcasted_iota(jnp.int32, (block, n), 1) >= lax.broadcasted_iota(jnp.int32, (block, n), 0) + lo
        u_ref[lo : lo + block, :] = jnp.where(keep, full[:, :n], 0.0)
        m_ref[lo : lo + block, :] = full[:, n:]
        if lo + block < n:
            a_ref[lo + block :, :] -= dot(full[:, lo + block : n], full, ((0,), (0,)), HIGH)


def fetch_and_reduce(
    tl_ref, pt_ref, t_hbm,
    t_out, pt_out, cr_out, u_out, m_out,
    wide, gx, gy, gz, aug, s1, l1, s2,
    t_sem, p_send, p_recv, g_send, g_recv, c_send, c_recv,
):
    width, active = pt_ref.shape[0], tl_ref.shape[0]
    n = 8 * width
    pair = 2 * width
    tiles = t_out.shape[0]
    spare = tiles - active
    part = t_out.shape[2] // 4
    r, c = lax.axis_index("row"), lax.axis_index("col")
    x, y, z, k = r // 4, lax.rem(r, 4), c // 2, lax.rem(c, 2)

    def along_x(d):
        return (lax.rem(x + d, 4) * 4 + y, c)

    def along_y(d):
        return (x * 4 + lax.rem(y + d, 4), c)

    def along_z(d):
        return (r, lax.rem(z + d, 4) * 2 + k)

    sibling = (r, z * 2 + 1 - k)

    barrier = pltpu.get_barrier_semaphore()
    partners = [f(d) for f in (along_x, along_y, along_z) for d in (1, 2, 3)] + [sibling]
    for partner in partners:
        pl.semaphore_signal(barrier, inc=1, device_id=partner, device_id_type=MESH)

    loads = []
    for i in range(6):
        copy = pltpu.make_async_copy(t_hbm.at[pl.ds(4 * i, 4)], t_out.at[pl.ds(4 * i, 4)], t_sem.at[i])
        copy.start()
        loads.append(copy)

    for j in range(active):
        pick = pt_ref[:, (j + spare) * TILE : (j + spare + 1) * TILE]
        for i in reversed(range(spare)):
            pick = jnp.where(tl_ref[j] == j + i, pt_ref[:, (j + i) * TILE : (j + i + 1) * TILE], pick)
        pt_out[z, k, :, j * TILE : (j + 1) * TILE] = pick
    pl.semaphore_wait(barrier, len(partners))

    def send(src, dst, send_sem, recv_sem, to):
        copy = pltpu.make_async_remote_copy(
            src_ref=src, dst_ref=dst, send_sem=send_sem, recv_sem=recv_sem, device_id=to, device_id_type=MESH
        )
        copy.start()
        return copy

    def finish_all(copies):
        for copy in copies:
            copy.wait()

    own = pt_out.at[z, k]
    near = send(own, own, p_send.at[0], p_recv.at[0], sibling)
    far = {d: send(own, own, p_send.at[d], p_recv.at[d], along_z(d)) for d in (1, 3, 2)}

    def source(d):
        return lax.rem(z + 4 - d, 4)

    def relay(d):
        far[d].wait_recv()
        block = pt_out.at[source(d), k]
        return send(block, block, p_send.at[3 + d], p_recv.at[3 + d], sibling)

    def lanes(d):
        return (along_x, along_y, x, y) if d in (0, 3) else (along_y, along_x, y, x)

    def cross(chunks):
        for d in chunks:
            for j in range(tiles):
                spread = jnp.zeros((2, width, TILE), BF16)
                for i in range(max(j - spare, 0), min(j, active - 1) + 1):
                    spread = jnp.where(tl_ref[i] == j, pt_out[source(d), :, :, i * TILE : (i + 1) * TILE], spread)
                wide[d, :, j * TILE : (j + 1) * TILE] = spread.reshape(pair, TILE)
        lhs = jnp.concatenate([wide[d] for d in chunks], axis=0)
        for t in range(4):
            rhs = t_out[:, :, t * part : (t + 1) * part].reshape(tiles * TILE, part)
            product = dot(lhs, rhs, ((1,), (0,))).astype(BF16)
            for i, d in enumerate(chunks):
                s1[d, t] = product[i * pair : (i + 1) * pair]
        for d in chunks:
            a, _, ma, _ = lanes(d)
            stage1[d] = [
                send(s1.at[d, lax.rem(ma + e, 4)], l1.at[d, e - 1], c_send.at[9 * d + e - 1], c_recv.at[9 * d + e - 1], a(e))
                for e in (2, 1, 3)
            ]

    def second(d):
        _, b, ma, mb = lanes(d)
        finish_all(stage1[d])
        total = s1[d, ma].astype(F32)
        for e in range(3):
            total = total + l1[d, e].astype(F32)
        s2[d, mb] = total.astype(BF16)
        stage2[d] = [
            send(s2.at[d, mb], s2.at[d, mb], c_send.at[9 * d + 2 + e], c_recv.at[9 * d + 2 + e], b(e)) for e in (2, 1, 3)
        ]

    def third(d):
        a, _, ma, _ = lanes(d)
        finish_all(stage2[d])
        total = s2[d, 0].astype(F32)
        for e in range(1, 4):
            total = total + s2[d, e].astype(F32)
        block = cr_out.at[source(d), ma]
        block[...] = total.astype(BF16)
        stage3.extend(send(block, block, c_send.at[9 * d + 5 + e], c_recv.at[9 * d + 5 + e], a(e)) for e in (2, 1, 3))

    stage1, stage2, stage3 = {}, {}, []
    near.wait_recv()
    finish_all(loads)
    cross((0,))
    relays = [relay(1), relay(3)]
    for copy in relays:
        copy.wait_recv()
    cross((1, 3))
    relays.append(relay(2))
    relays[2].wait_recv()

    everything = pt_out[...].reshape(n, active * TILE)
    half = pt_out[pl.ds(2 * k, 2)].reshape(n // 2, active * TILE)
    gx[x] = dot(half, everything, ((1,), (1,))).astype(BF16)
    over_x = [send(gx.at[x], gx.at[x], g_send.at[e - 1], g_recv.at[e - 1], along_x(e)) for e in (2, 1, 3)]
    cross((2,))

    second(0)
    finish_all(over_x)
    gy[y] = (gx[0].astype(F32) + gx[1].astype(F32) + gx[2].astype(F32) + gx[3].astype(F32)).astype(BF16)
    over_y = [send(gy.at[y], gy.at[y], g_send.at[2 + e], g_recv.at[2 + e], along_y(e)) for e in (2, 1, 3)]
    second(1)
    second(3)
    second(2)
    finish_all(over_y)
    gz[k] = gy[0].astype(F32) + gy[1].astype(F32) + gy[2].astype(F32) + gy[3].astype(F32)
    swap = send(gz.at[k], gz.at[k], g_send.at[6], g_recv.at[6], sibling)
    third(0)
    swap.wait()
    aug[:, :n] = gz[...].reshape(n, n)
    eye = lax.broadcasted_iota(jnp.int32, (n, n), 0) == lax.broadcasted_iota(jnp.int32, (n, n), 1)
    aug[:, n:] = jnp.where(eye, 1.0, 0.0)
    steps = factor(aug, u_out, m_out, n, 32)
    for _ in range(4):
        next(steps)
    third(1)
    third(3)
    for _ in range(4):
        next(steps)
    third(2)
    for _ in steps:
        pass
    finish_all(stage3)
    near.wait_send()
    for copy in relays:
        copy.wait_send()
    for copy in far.values():
        copy.wait_send()


def finish(tl_ref, t_ref, pt_ref, cr_ref, u_ref, m_ref, tri_ref, top_hbm, up_hbm, coeff, tops, outs, top_sem, out_sem):
    n = m_ref.shape[0]
    active = tl_ref.shape[0]
    tri_ref[...] = u_ref[...]
    m = m_ref[...]
    mh = m.astype(BF16)
    ml = (m - mh.astype(F32)).astype(BF16)
    copies = []
    for q in range(4):
        part = cr_ref[:, q].reshape(n, 512)
        top = dot(mh, part, ((1,), (0,))) + dot(ml, part, ((1,), (0,)))
        tops[q] = top.T
        copy = pltpu.make_async_copy(tops.at[q], top_hbm.at[pl.ds(q * 512, 512)], top_sem.at[q])
        copy.start()
        copies.append(copy)
        tb = top.astype(BF16)
        coeff[:, q * 512 : (q + 1) * 512] = (dot(mh, tb, ((0,), (0,))) + dot(ml, tb, ((0,), (0,)))).astype(BF16)
    pending = [None] * 3
    for i in range(active // 2):
        slot = i % 3
        if pending[slot] is not None:
            pending[slot].wait()
        cols = pt_ref[:, :, :, i * 256 : (i + 1) * 256].reshape(n, 256)
        product = dot(cols, coeff[...], ((0,), (0,)))
        outs[slot, :128] = (t_ref[tl_ref[2 * i]].astype(F32) - product[:128]).astype(BF16)
        outs[slot, 128:] = (t_ref[tl_ref[2 * i + 1]].astype(F32) - product[128:]).astype(BF16)
        copy = pltpu.make_async_copy(outs.at[slot], up_hbm.at[pl.ds(i * 256, 256)], out_sem.at[slot])
        copy.start()
        pending[slot] = copy
    for copy in pending + copies:
        copy.wait()


def call_finish(tile_list, t, pt, cr, u, m):
    vmem = pl.BlockSpec(memory_space=pltpu.VMEM)
    smem = pl.BlockSpec(memory_space=pltpu.SMEM)
    anywhere = pl.BlockSpec(memory_space=pl.ANY)
    dma = pltpu.SemaphoreType.DMA
    n = m.shape[0]
    cols = t.shape[2]
    active = tile_list.shape[0]
    return pl.pallas_call(
        finish,
        out_shape=(
            jax.ShapeDtypeStruct((n, n), F32),
            jax.ShapeDtypeStruct((cols, n), F32),
            jax.ShapeDtypeStruct((active * TILE, cols), BF16),
        ),
        in_specs=[smem] + [vmem] * 5,
        out_specs=[vmem, anywhere, anywhere],
        scratch_shapes=[
            pltpu.VMEM((n, cols), BF16),
            pltpu.VMEM((4, cols // 4, n), F32),
            pltpu.VMEM((3, 2 * TILE, cols), BF16),
            dma((4,)),
            dma((3,)),
        ],
        compiler_params=pltpu.CompilerParams(vmem_limit_bytes=24 * 2**20),
    )(tile_list, t, pt, cr, u, m)


def local(panel, trailing, tile_list):
    rows, width = panel.shape
    cols = trailing.shape[1]
    active = tile_list.shape[0]
    tiles = rows // TILE
    n = 8 * width
    vmem = pl.BlockSpec(memory_space=pltpu.VMEM)
    smem = pl.BlockSpec(memory_space=pltpu.SMEM)
    hbm = pl.BlockSpec(memory_space=pltpu.HBM)
    dma = pltpu.SemaphoreType.DMA
    t, pt, cr, u, m = pl.pallas_call(
        fetch_and_reduce,
        out_shape=(
            pltpu.VMEM((tiles, TILE, cols), BF16),
            pltpu.VMEM((4, 2, width, active * TILE), BF16),
            pltpu.VMEM((4, 4, 2 * width, cols // 4), BF16),
            pltpu.VMEM((n, n), F32),
            pltpu.VMEM((n, n), F32),
        ),
        in_specs=[smem, vmem, hbm],
        out_specs=[vmem] * 5,
        scratch_shapes=[
            pltpu.VMEM((4, 2 * width, rows), BF16),
            pltpu.VMEM((4, n // 2, n), BF16),
            pltpu.VMEM((4, n // 2, n), BF16),
            pltpu.VMEM((2, n // 2, n), F32),
            pltpu.VMEM((n, 2 * n), F32),
            pltpu.VMEM((4, 4, 2 * width, cols // 4), BF16),
            pltpu.VMEM((4, 3, 2 * width, cols // 4), BF16),
            pltpu.VMEM((4, 4, 2 * width, cols // 4), BF16),
            dma((6,)),
            dma((7,)),
            dma((7,)),
            dma((7,)),
            dma((7,)),
            dma((36,)),
            dma((36,)),
        ],
        compiler_params=pltpu.CompilerParams(collective_id=0, has_side_effects=True, vmem_limit_bytes=24 * 2**20),
    )(tile_list, panel.T, pltpu.with_memory_space_constraint(trailing.reshape(tiles, TILE, cols), pltpu.HBM))
    return call_finish(tile_list, t, pt, cr, u, m)


def solution(mesh):
    return jax.shard_map(
        local,
        mesh=mesh,
        in_specs=(P("row", "col"), P("row", "col"), P("row")),
        out_specs=(P(), P("col", None), P("row", "col")),
        check_vma=False,
    )
```

```python
import functools

import jax
import jax.numpy as jnp
from jax import lax
from jax.experimental import pallas as pl
from jax.experimental.pallas import tpu as pltpu
from jax.sharding import PartitionSpec as P

TILE = 128
MESH = pl.DeviceIdType.MESH
F32 = jnp.float32
BF16 = jnp.bfloat16
HIGH = lax.Precision.HIGHEST


def dot(a, b, dims, precision=None):
    return lax.dot_general(a, b, (dims, ((), ())), precision=precision, preferred_element_type=F32)


def spread_entries(d, p):
    a, low, inv = {}, {}, {}
    for i in range(p):
        for j in range(i + 1):
            a[i, j] = jnp.broadcast_to(d[j : j + 1, i : i + 1], (8, 128))
    for j in range(p):
        inv[j, j] = lax.rsqrt(a[j, j])
        for i in range(j, p):
            low[i, j] = a[i, j] * inv[j, j]
        for k in range(j + 1, p):
            for i in range(k, p):
                a[i, k] = a[i, k] - low[i, j] * low[k, j]
    for i in range(p):
        for j in range(i):
            total = sum(low[i, k] * inv[k, j] for k in range(j, i))
            inv[i, j] = -total * inv[i, i]
    return inv


def factor(a_ref, u_ref, m_ref, n, block, p=8):
    wide = 2 * n // 128
    rows = lax.broadcasted_iota(jnp.int32, (8, 128), 0)

    def across(column):
        return jnp.concatenate([column] * wide, axis=1)

    for lo in range(0, n, block):
        groups = [a_ref[lo + i : lo + i + p, :] for i in range(0, block, p)]
        done = []
        for g in range(block // p):
            at = lo + g * p
            inv = spread_entries(groups[g][:, at : at + p], p)
            u = None
            for j in range(p):
                column = jnp.zeros((8, 128), F32)
                for i in range(j, p):
                    column = jnp.where(rows == i, inv[i, j], column)
                term = across(column) * groups[g][j : j + 1, :]
                u = term if u is None else u + term
            done.append(u)
            for h in range(g + 1, block // p):
                left = [jnp.broadcast_to(groups[h][:, at + q : at + q + 1], (8, 128)) for q in range(p)]
                rest = groups[h]
                for j in range(p):
                    column = sum(left[q] * inv[j, q] for q in range(j + 1))
                    rest = rest - across(column) * u[j : j + 1, :]
                groups[h] = rest
            yield
        full = jnp.concatenate(done, axis=0)
        keep = lax.broadcasted_iota(jnp.int32, (block, n), 1) >= lax.broadcasted_iota(jnp.int32, (block, n), 0) + lo
        u_ref[lo : lo + block, :] = jnp.where(keep, full[:, :n], 0.0)
        m_ref[lo : lo + block, :] = full[:, n:]
        if lo + block < n:
            a_ref[lo + block :, :] -= dot(full[:, lo + block : n], full, ((0,), (0,)), HIGH)


def fetch_and_reduce(
    tl_hbm, pt_hbm, t_hbm,
    t_out, p_out, cr_out, u_out, m_out,
    tl_ref, pt_ref, pt_out, wide, gx, gy, gz, aug, s1, l1, s2,
    t_sem, p_send, p_recv, g_send, g_recv, c_send, c_recv,
):
    width, active = pt_ref.shape[0], tl_ref.shape[0]
    n = 8 * width
    pair = 2 * width
    tiles = t_out.shape[0]
    spare = tiles - active
    part = t_out.shape[2] // 8
    r, c = lax.axis_index("row"), lax.axis_index("col")
    x, y, z, k = r // 4, lax.rem(r, 4), c // 2, lax.rem(c, 2)

    def along_x(d):
        return (lax.rem(x + d, 4) * 4 + y, c)

    def along_y(d):
        return (x * 4 + lax.rem(y + d, 4), c)

    def along_z(d):
        return (r, lax.rem(z + d, 4) * 2 + k)

    sibling = (r, z * 2 + 1 - k)

    barrier = pltpu.get_barrier_semaphore()
    partners = [f(d) for f in (along_x, along_y, along_z) for d in (1, 2, 3)] + [sibling]
    for partner in partners:
        pl.semaphore_signal(barrier, inc=1, device_id=partner, device_id_type=MESH)

    early = [pltpu.make_async_copy(tl_hbm, tl_ref, t_sem.at[6]), pltpu.make_async_copy(pt_hbm, pt_ref, t_sem.at[7])]
    for copy in early:
        copy.start()
    loads = []
    for i in range(6):
        copy = pltpu.make_async_copy(t_hbm.at[pl.ds(4 * i, 4)], t_out.at[pl.ds(4 * i, 4)], t_sem.at[i])
        copy.start()
        loads.append(copy)

    for copy in early:
        copy.wait()
    for j in range(active):
        pick = pt_ref[:, (j + spare) * TILE : (j + spare + 1) * TILE]
        for i in reversed(range(spare)):
            pick = jnp.where(tl_ref[j] == j + i, pt_ref[:, (j + i) * TILE : (j + i + 1) * TILE], pick)
        pt_out[z, k, :, j * TILE : (j + 1) * TILE] = pick
    pl.semaphore_wait(barrier, len(partners))

    def send(src, dst, send_sem, recv_sem, to):
        copy = pltpu.make_async_remote_copy(
            src_ref=src, dst_ref=dst, send_sem=send_sem, recv_sem=recv_sem, device_id=to, device_id_type=MESH
        )
        copy.start()
        return copy

    def finish_all(copies):
        for copy in copies:
            copy.wait()

    own = pt_out.at[z, k]
    near = send(own, own, p_send.at[0], p_recv.at[0], sibling)
    far = {d: send(own, own, p_send.at[d], p_recv.at[d], along_z(d)) for d in (1, 3, 2)}

    def source(d):
        return lax.rem(z + 4 - d, 4)

    def relay(d):
        far[d].wait_recv()
        block = pt_out.at[source(d), k]
        return send(block, block, p_send.at[3 + d], p_recv.at[3 + d], sibling)

    def lanes(h):
        return (along_x, along_y, x, y) if h == 0 else (along_y, along_x, y, x)

    def cross(chunks):
        for d in chunks:
            for j in range(tiles):
                spread = jnp.zeros((2, width, TILE), BF16)
                for i in range(max(j - spare, 0), min(j, active - 1) + 1):
                    spread = jnp.where(tl_ref[i] == j, pt_out[source(d), :, :, i * TILE : (i + 1) * TILE], spread)
                wide[d, :, j * TILE : (j + 1) * TILE] = spread.reshape(pair, TILE)
        lhs = jnp.concatenate([wide[d] for d in chunks], axis=0)
        for h in range(2):
            for t in range(2):
                at = (2 * h + t) * 2 * part
                rhs = t_out[:, :, at : at + 2 * part].reshape(tiles * TILE, 2 * part)
                product = dot(lhs, rhs, ((1,), (0,))).astype(BF16)
                for i, d in enumerate(chunks):
                    s1[d, h, 2 * t] = product[i * pair : (i + 1) * pair, :part]
                    s1[d, h, 2 * t + 1] = product[i * pair : (i + 1) * pair, part:]
            a, _, ma, _ = lanes(h)
            for d in chunks:
                sem = 9 * (2 * d + h) - 1
                stage1[d, h] = [
                    send(s1.at[d, h, lax.rem(ma + e, 4)], l1.at[d, h, e - 1], c_send.at[sem + e], c_recv.at[sem + e], a(e))
                    for e in (2, 1, 3)
                ]

    def second(d):
        for h in range(2):
            _, b, ma, mb = lanes(h)
            finish_all(stage1[d, h])
            total = s1[d, h, ma].astype(F32)
            for e in range(3):
                total = total + l1[d, h, e].astype(F32)
            block = s2.at[d, h, mb]
            block[...] = total.astype(BF16)
            sem = 9 * (2 * d + h) + 2
            stage2[d, h] = [send(block, block, c_send.at[sem + e], c_recv.at[sem + e], b(e)) for e in (2, 1, 3)]

    def third(d):
        for h in range(2):
            a, _, ma, _ = lanes(h)
            finish_all(stage2[d, h])
            total = s2[d, h, 0].astype(F32)
            for e in range(1, 4):
                total = total + s2[d, h, e].astype(F32)
            block = cr_out.at[source(d), h, ma]
            block[...] = total.astype(BF16)
            sem = 9 * (2 * d + h) + 5
            stage3.extend(send(block, block, c_send.at[sem + e], c_recv.at[sem + e], a(e)) for e in (2, 1, 3))

    stage1, stage2, stage3 = {}, {}, []
    near.wait_recv()
    finish_all(loads)
    cross((0,))
    relays = [relay(1), relay(3)]
    for copy in relays:
        copy.wait_recv()
    cross((1, 3))
    second(0)
    relays.append(relay(2))
    relays[2].wait_recv()

    everything = pt_out[...].reshape(n, active * TILE)
    half = pt_out[pl.ds(2 * k, 2)].reshape(n // 2, active * TILE)
    gx[x] = dot(half, everything, ((1,), (1,))).astype(BF16)
    over_x = [send(gx.at[x], gx.at[x], g_send.at[e - 1], g_recv.at[e - 1], along_x(e)) for e in (2, 1, 3)]
    cross((2,))

    for i in range(0, active * TILE, 2 * TILE):
        p_out[i : i + 2 * TILE, :] = pt_out[:, :, :, i : i + 2 * TILE].reshape(n, 2 * TILE).T
    second(1)
    second(3)
    finish_all(over_x)
    gy[y] = (gx[0].astype(F32) + gx[1].astype(F32) + gx[2].astype(F32) + gx[3].astype(F32)).astype(BF16)
    over_y = [send(gy.at[y], gy.at[y], g_send.at[2 + e], g_recv.at[2 + e], along_y(e)) for e in (2, 1, 3)]
    second(2)
    third(0)
    finish_all(over_y)
    gz[k] = gy[0].astype(F32) + gy[1].astype(F32) + gy[2].astype(F32) + gy[3].astype(F32)
    swap = send(gz.at[k], gz.at[k], g_send.at[6], g_recv.at[6], sibling)
    third(1)
    third(3)
    swap.wait()
    aug[:, :n] = gz[...].reshape(n, n)
    eye = lax.broadcasted_iota(jnp.int32, (n, n), 0) == lax.broadcasted_iota(jnp.int32, (n, n), 1)
    aug[:, n:] = jnp.where(eye, 1.0, 0.0)
    steps = factor(aug, u_out, m_out, n, 32)
    for _ in range(4):
        next(steps)
    third(2)
    for _ in steps:
        pass
    finish_all(stage3)
    near.wait_send()
    for copy in relays:
        copy.wait_send()
    for copy in far.values():
        copy.wait_send()


def finish(tl_ref, t_ref, p_ref, cr_ref, u_ref, m_ref, tri_ref, top_hbm, up_hbm, tops, outs, top_sem, out_sem):
    n = m_ref.shape[0]
    active = tl_ref.shape[0]
    part = t_ref.shape[2] // 4
    tri_ref[...] = u_ref[...]
    m = m_ref[...]
    mh = m.astype(BF16)
    ml = (m - mh.astype(F32)).astype(BF16)
    copies = []
    for q in range(4):
        cols = slice(q * part, (q + 1) * part)
        blocks = [cr_ref[:, q // 2, 2 * (q % 2) + e].reshape(n, part // 2) for e in range(2)]
        cross = jnp.concatenate(blocks, axis=1)
        top = dot(mh, cross, ((1,), (0,))) + dot(ml, cross, ((1,), (0,)))
        coeff = dot(mh, top.astype(BF16), ((0,), (0,))).astype(BF16)
        tops[q] = top.T
        copy = pltpu.make_async_copy(tops.at[q], top_hbm.at[pl.ds(q * part, part)], top_sem.at[q])
        copy.start()
        copies.append(copy)
        for i in range(active // 2):
            rows = slice(2 * i * TILE, 2 * (i + 1) * TILE)
            product = dot(p_ref[rows, :], coeff, ((1,), (0,)))
            old = jnp.concatenate([t_ref[tl_ref[2 * i + e], :, cols] for e in range(2)], axis=0)
            outs[rows, cols] = (old.astype(F32) - product).astype(BF16)
            copy = pltpu.make_async_copy(outs.at[rows, cols], up_hbm.at[rows, cols], out_sem.at[q, i])
            copy.start()
            copies.append(copy)
    for copy in copies:
        copy.wait()


def call_finish(tile_list, t, p, cr, u, m):
    vmem = pl.BlockSpec(memory_space=pltpu.VMEM)
    smem = pl.BlockSpec(memory_space=pltpu.SMEM)
    anywhere = pl.BlockSpec(memory_space=pl.ANY)
    n = m.shape[0]
    cols = t.shape[2]
    active = tile_list.shape[0]
    return pl.pallas_call(
        finish,
        out_shape=(
            jax.ShapeDtypeStruct((n, n), F32),
            jax.ShapeDtypeStruct((cols, n), F32),
            jax.ShapeDtypeStruct((active * TILE, cols), BF16),
        ),
        in_specs=[smem] + [vmem] * 5,
        out_specs=[vmem, anywhere, anywhere],
        scratch_shapes=[
            pltpu.VMEM((4, cols // 4, n), F32),
            pltpu.VMEM((active * TILE, cols), BF16),
            pltpu.SemaphoreType.DMA((4,)),
            pltpu.SemaphoreType.DMA((4, active // 2)),
        ],
        compiler_params=pltpu.CompilerParams(vmem_limit_bytes=24 * 2**20),
    )(tile_list, t, p, cr, u, m)


def local(panel, trailing, tile_list):
    rows, width = panel.shape
    cols = trailing.shape[1]
    active = tile_list.shape[0]
    tiles = rows // TILE
    n = 8 * width
    vmem = pl.BlockSpec(memory_space=pltpu.VMEM)
    hbm = pl.BlockSpec(memory_space=pltpu.HBM)
    dma = pltpu.SemaphoreType.DMA
    t, p, cr, u, m = pl.pallas_call(
        fetch_and_reduce,
        out_shape=(
            pltpu.VMEM((tiles, TILE, cols), BF16),
            pltpu.VMEM((active * TILE, n), BF16),
            pltpu.VMEM((4, 2, 4, 2 * width, cols // 8), BF16),
            pltpu.VMEM((n, n), F32),
            pltpu.VMEM((n, n), F32),
        ),
        in_specs=[hbm] * 3,
        out_specs=[vmem] * 5,
        scratch_shapes=[
            pltpu.SMEM((active,), jnp.int32),
            pltpu.VMEM((width, rows), BF16),
            pltpu.VMEM((4, 2, width, active * TILE), BF16),
            pltpu.VMEM((4, 2 * width, rows), BF16),
            pltpu.VMEM((4, n // 2, n), BF16),
            pltpu.VMEM((4, n // 2, n), BF16),
            pltpu.VMEM((2, n // 2, n), F32),
            pltpu.VMEM((n, 2 * n), F32),
            pltpu.VMEM((4, 2, 4, 2 * width, cols // 8), BF16),
            pltpu.VMEM((4, 2, 3, 2 * width, cols // 8), BF16),
            pltpu.VMEM((4, 2, 4, 2 * width, cols // 8), BF16),
            dma((8,)),
            dma((7,)),
            dma((7,)),
            dma((7,)),
            dma((7,)),
            dma((72,)),
            dma((72,)),
        ],
        compiler_params=pltpu.CompilerParams(collective_id=0, has_side_effects=True, vmem_limit_bytes=24 * 2**20),
    )(
        *(
            pltpu.with_memory_space_constraint(a, pltpu.HBM)
            for a in (tile_list, panel.T, trailing.reshape(tiles, TILE, cols))
        )
    )
    return call_finish(tile_list, t, p, cr, u, m)


def solution(mesh):
    return jax.shard_map(
        local,
        mesh=mesh,
        in_specs=(P("row", "col"), P("row", "col"), P("row")),
        out_specs=(P(), P("col", None), P("row", "col")),
        check_vma=False,
    )
```

```python
import functools

import jax
import jax.numpy as jnp
from jax import lax
from jax.experimental import pallas as pl
from jax.experimental.pallas import tpu as pltpu
from jax.sharding import PartitionSpec as P

TILE = 128
MESH = pl.DeviceIdType.MESH
F32 = jnp.float32
BF16 = jnp.bfloat16
HIGH = lax.Precision.HIGHEST


def dot(a, b, dims, precision=None):
    return lax.dot_general(a, b, (dims, ((), ())), precision=precision, preferred_element_type=F32)


def spread_entries(d, p):
    a, low, inv = {}, {}, {}
    for i in range(p):
        for j in range(i + 1):
            a[i, j] = jnp.broadcast_to(d[j : j + 1, i : i + 1], (8, 128))
    for j in range(p):
        inv[j, j] = lax.rsqrt(a[j, j])
        for i in range(j, p):
            low[i, j] = a[i, j] * inv[j, j]
        for k in range(j + 1, p):
            for i in range(k, p):
                a[i, k] = a[i, k] - low[i, j] * low[k, j]
    for i in range(p):
        for j in range(i):
            total = sum(low[i, k] * inv[k, j] for k in range(j, i))
            inv[i, j] = -total * inv[i, i]
    return inv


def factor(a_ref, u_ref, m_ref, n, block, p=8):
    lane = 128
    count = 2 * n // lane
    rows = lax.broadcasted_iota(jnp.int32, (8, lane), 0)

    for lo in range(0, n, block):
        groups = [[a_ref[lo + i : lo + i + p, w * lane : (w + 1) * lane] for w in range(count)] for i in range(0, block, p)]
        done = []
        for g in range(block // p):
            at = lo + g * p
            own, off = at // lane, at % lane
            live = [w for w in range(count) if (w >= own if w < count // 2 else w - count // 2 <= own)]
            inv = spread_entries(groups[g][own][:, off : off + p], p)
            columns = []
            for j in range(p):
                column = jnp.zeros((8, lane), F32)
                for i in range(j, p):
                    column = jnp.where(rows == i, inv[i, j], column)
                columns.append(column)
            u = [jnp.zeros((p, lane), F32)] * count
            for w in live:
                u[w] = sum(columns[j] * groups[g][w][j : j + 1, :] for j in range(p))
            done.append(jnp.concatenate(u, axis=1))
            for h in range(g + 1, block // p):
                left = [jnp.broadcast_to(groups[h][own][:, off + q : off + q + 1], (8, lane)) for q in range(p)]
                lower = [sum(left[q] * inv[j, q] for q in range(j + 1)) for j in range(p)]
                for w in live:
                    rest = groups[h][w]
                    for j in range(p):
                        rest = rest - lower[j] * u[w][j : j + 1, :]
                    groups[h][w] = rest
            yield
        full = jnp.concatenate(done, axis=0)
        keep = lax.broadcasted_iota(jnp.int32, (block, n), 1) >= lax.broadcasted_iota(jnp.int32, (block, n), 0) + lo
        u_ref[lo : lo + block, :] = jnp.where(keep, full[:, :n], 0.0)
        m_ref[lo : lo + block, :] = full[:, n:]
        first = lo + block
        if first < n:
            cols = slice(first // lane * lane, n + ((first - 1) // lane + 1) * lane)
            spans = [(first, first + block), (first + block, n)] if first + block < n else [(first, n)]
            for a, b in spans:
                a_ref[a:b, cols] -= dot(full[:, a:b], full[:, cols], ((0,), (0,)), HIGH)


def fetch_and_reduce(
    tl_hbm, pt_hbm, t_hbm,
    t_out, p_out, cr_out, u_out, m_out,
    tl_ref, pt_ref, pt_out, wide, gx, gy, gz, aug, s1, l1, s2,
    t_sem, p_send, p_recv, g_send, g_recv, c_send, c_recv,
):
    width, active = pt_ref.shape[0], tl_ref.shape[0]
    n = 8 * width
    pair = 2 * width
    tiles = t_out.shape[0]
    spare = tiles - active
    part = t_out.shape[2] // 8
    r, c = lax.axis_index("row"), lax.axis_index("col")
    x, y, z, k = r // 4, lax.rem(r, 4), c // 2, lax.rem(c, 2)

    def along_x(d):
        return (lax.rem(x + d, 4) * 4 + y, c)

    def along_y(d):
        return (x * 4 + lax.rem(y + d, 4), c)

    def along_z(d):
        return (r, lax.rem(z + d, 4) * 2 + k)

    sibling = (r, z * 2 + 1 - k)

    barrier = pltpu.get_barrier_semaphore()
    partners = [f(d) for f in (along_x, along_y, along_z) for d in (1, 2, 3)] + [sibling]
    for partner in partners:
        pl.semaphore_signal(barrier, inc=1, device_id=partner, device_id_type=MESH)

    early = [pltpu.make_async_copy(tl_hbm, tl_ref, t_sem.at[6]), pltpu.make_async_copy(pt_hbm, pt_ref, t_sem.at[7])]
    for copy in early:
        copy.start()
    loads = []
    for i in range(6):
        copy = pltpu.make_async_copy(t_hbm.at[pl.ds(4 * i, 4)], t_out.at[pl.ds(4 * i, 4)], t_sem.at[i])
        copy.start()
        loads.append(copy)

    for copy in early:
        copy.wait()
    for j in range(active):
        pick = pt_ref[:, (j + spare) * TILE : (j + spare + 1) * TILE]
        for i in reversed(range(spare)):
            pick = jnp.where(tl_ref[j] == j + i, pt_ref[:, (j + i) * TILE : (j + i + 1) * TILE], pick)
        pt_out[z, k, :, j * TILE : (j + 1) * TILE] = pick
    pl.semaphore_wait(barrier, len(partners))

    def send(src, dst, send_sem, recv_sem, to):
        copy = pltpu.make_async_remote_copy(
            src_ref=src, dst_ref=dst, send_sem=send_sem, recv_sem=recv_sem, device_id=to, device_id_type=MESH
        )
        copy.start()
        return copy

    def finish_all(copies):
        for copy in copies:
            copy.wait()

    own = pt_out.at[z, k]
    near = send(own, own, p_send.at[0], p_recv.at[0], sibling)
    far = {d: send(own, own, p_send.at[d], p_recv.at[d], along_z(d)) for d in (1, 3, 2)}

    def source(d):
        return lax.rem(z + 4 - d, 4)

    def relay(d):
        far[d].wait_recv()
        block = pt_out.at[source(d), k]
        return send(block, block, p_send.at[3 + d], p_recv.at[3 + d], sibling)

    def lanes(h):
        return (along_x, along_y, x, y) if h == 0 else (along_y, along_x, y, x)

    def cross(chunks):
        for d in chunks:
            for j in range(tiles):
                spread = jnp.zeros((2, width, TILE), BF16)
                for i in range(max(j - spare, 0), min(j, active - 1) + 1):
                    spread = jnp.where(tl_ref[i] == j, pt_out[source(d), :, :, i * TILE : (i + 1) * TILE], spread)
                wide[d, :, j * TILE : (j + 1) * TILE] = spread.reshape(pair, TILE)
        lhs = jnp.concatenate([wide[d] for d in chunks], axis=0)
        for h in range(2):
            for t in range(2):
                at = (2 * h + t) * 2 * part
                rhs = t_out[:, :, at : at + 2 * part].reshape(tiles * TILE, 2 * part)
                product = dot(lhs, rhs, ((1,), (0,))).astype(BF16)
                for i, d in enumerate(chunks):
                    s1[d, h, 2 * t] = product[i * pair : (i + 1) * pair, :part]
                    s1[d, h, 2 * t + 1] = product[i * pair : (i + 1) * pair, part:]
            a, _, ma, _ = lanes(h)
            for d in chunks:
                sem = 9 * (2 * d + h) - 1
                stage1[d, h] = [
                    send(s1.at[d, h, lax.rem(ma + e, 4)], l1.at[d, h, e - 1], c_send.at[sem + e], c_recv.at[sem + e], a(e))
                    for e in (2, 1, 3)
                ]

    def second(d):
        for h in range(2):
            _, b, ma, mb = lanes(h)
            finish_all(stage1[d, h])
            total = s1[d, h, ma].astype(F32)
            for e in range(3):
                total = total + l1[d, h, e].astype(F32)
            block = s2.at[d, h, mb]
            block[...] = total.astype(BF16)
            sem = 9 * (2 * d + h) + 2
            stage2[d, h] = [send(block, block, c_send.at[sem + e], c_recv.at[sem + e], b(e)) for e in (2, 1, 3)]

    def third(d):
        for h in range(2):
            a, _, ma, _ = lanes(h)
            finish_all(stage2[d, h])
            total = s2[d, h, 0].astype(F32)
            for e in range(1, 4):
                total = total + s2[d, h, e].astype(F32)
            block = cr_out.at[source(d), h, ma]
            block[...] = total.astype(BF16)
            sem = 9 * (2 * d + h) + 5
            stage3.extend(send(block, block, c_send.at[sem + e], c_recv.at[sem + e], a(e)) for e in (2, 1, 3))

    stage1, stage2, stage3 = {}, {}, []
    near.wait_recv()
    finish_all(loads)
    cross((0,))
    relays = [relay(1), relay(3)]
    for copy in relays:
        copy.wait_recv()
    cross((1, 3))
    second(0)
    relays.append(relay(2))
    relays[2].wait_recv()

    everything = pt_out[...].reshape(n, active * TILE)
    half = pt_out[pl.ds(2 * k, 2)].reshape(n // 2, active * TILE)
    gx[x] = dot(half, everything, ((1,), (1,))).astype(BF16)
    over_x = [send(gx.at[x], gx.at[x], g_send.at[e - 1], g_recv.at[e - 1], along_x(e)) for e in (2, 1, 3)]
    cross((2,))

    for i in range(0, active * TILE, 2 * TILE):
        p_out[i : i + 2 * TILE, :] = pt_out[:, :, :, i : i + 2 * TILE].reshape(n, 2 * TILE).T
    finish_all(over_x)
    gy[y] = (gx[0].astype(F32) + gx[1].astype(F32) + gx[2].astype(F32) + gx[3].astype(F32)).astype(BF16)
    over_y = [send(gy.at[y], gy.at[y], g_send.at[2 + e], g_recv.at[2 + e], along_y(e)) for e in (2, 1, 3)]
    second(1)
    second(3)
    second(2)
    finish_all(over_y)
    gz[k] = gy[0].astype(F32) + gy[1].astype(F32) + gy[2].astype(F32) + gy[3].astype(F32)
    swap = send(gz.at[k], gz.at[k], g_send.at[6], g_recv.at[6], sibling)
    third(0)
    swap.wait()
    aug[:, :n] = gz[...].reshape(n, n)
    eye = lax.broadcasted_iota(jnp.int32, (n, n), 0) == lax.broadcasted_iota(jnp.int32, (n, n), 1)
    aug[:, n:] = jnp.where(eye, 1.0, 0.0)
    steps = factor(aug, u_out, m_out, n, 32)
    for _ in range(3):
        next(steps)
    third(1)
    third(3)
    for _ in range(6):
        next(steps)
    third(2)
    for _ in steps:
        pass
    finish_all(stage3)
    near.wait_send()
    for copy in relays:
        copy.wait_send()
    for copy in far.values():
        copy.wait_send()


def finish(tl_ref, t_ref, p_ref, cr_ref, u_ref, m_ref, tri_ref, top_hbm, up_hbm, tops, outs, top_sem, out_sem):
    n = m_ref.shape[0]
    active = tl_ref.shape[0]
    part = t_ref.shape[2] // 4
    tri_ref[...] = u_ref[...]
    m = m_ref[...]
    mh = m.astype(BF16)
    ml = (m - mh.astype(F32)).astype(BF16)
    copies = []
    for q in range(4):
        cols = slice(q * part, (q + 1) * part)
        blocks = [cr_ref[:, q // 2, 2 * (q % 2) + e].reshape(n, part // 2) for e in range(2)]
        cross = jnp.concatenate(blocks, axis=1)
        top = dot(mh, cross, ((1,), (0,))) + dot(ml, cross, ((1,), (0,)))
        coeff = dot(mh, top.astype(BF16), ((0,), (0,))).astype(BF16)
        tops[q] = top.T
        copy = pltpu.make_async_copy(tops.at[q], top_hbm.at[pl.ds(q * part, part)], top_sem.at[q])
        copy.start()
        copies.append(copy)
        for i in range(active // 2):
            rows = slice(2 * i * TILE, 2 * (i + 1) * TILE)
            product = dot(p_ref[rows, :], coeff, ((1,), (0,)))
            old = jnp.concatenate([t_ref[tl_ref[2 * i + e], :, cols] for e in range(2)], axis=0)
            outs[rows, cols] = (old.astype(F32) - product).astype(BF16)
            copy = pltpu.make_async_copy(outs.at[rows, cols], up_hbm.at[rows, cols], out_sem.at[q, i])
            copy.start()
            copies.append(copy)
    for copy in copies:
        copy.wait()


def call_finish(tile_list, t, p, cr, u, m):
    vmem = pl.BlockSpec(memory_space=pltpu.VMEM)
    smem = pl.BlockSpec(memory_space=pltpu.SMEM)
    anywhere = pl.BlockSpec(memory_space=pl.ANY)
    n = m.shape[0]
    cols = t.shape[2]
    active = tile_list.shape[0]
    return pl.pallas_call(
        finish,
        out_shape=(
            jax.ShapeDtypeStruct((n, n), F32),
            jax.ShapeDtypeStruct((cols, n), F32),
            jax.ShapeDtypeStruct((active * TILE, cols), BF16),
        ),
        in_specs=[smem] + [vmem] * 5,
        out_specs=[vmem, anywhere, anywhere],
        scratch_shapes=[
            pltpu.VMEM((4, cols // 4, n), F32),
            pltpu.VMEM((active * TILE, cols), BF16),
            pltpu.SemaphoreType.DMA((4,)),
            pltpu.SemaphoreType.DMA((4, active // 2)),
        ],
        compiler_params=pltpu.CompilerParams(vmem_limit_bytes=24 * 2**20),
    )(tile_list, t, p, cr, u, m)


def local(panel, trailing, tile_list):
    rows, width = panel.shape
    cols = trailing.shape[1]
    active = tile_list.shape[0]
    tiles = rows // TILE
    n = 8 * width
    vmem = pl.BlockSpec(memory_space=pltpu.VMEM)
    hbm = pl.BlockSpec(memory_space=pltpu.HBM)
    dma = pltpu.SemaphoreType.DMA
    t, p, cr, u, m = pl.pallas_call(
        fetch_and_reduce,
        out_shape=(
            pltpu.VMEM((tiles, TILE, cols), BF16),
            pltpu.VMEM((active * TILE, n), BF16),
            pltpu.VMEM((4, 2, 4, 2 * width, cols // 8), BF16),
            pltpu.VMEM((n, n), F32),
            pltpu.VMEM((n, n), F32),
        ),
        in_specs=[hbm] * 3,
        out_specs=[vmem] * 5,
        scratch_shapes=[
            pltpu.SMEM((active,), jnp.int32),
            pltpu.VMEM((width, rows), BF16),
            pltpu.VMEM((4, 2, width, active * TILE), BF16),
            pltpu.VMEM((4, 2 * width, rows), BF16),
            pltpu.VMEM((4, n // 2, n), BF16),
            pltpu.VMEM((4, n // 2, n), BF16),
            pltpu.VMEM((2, n // 2, n), F32),
            pltpu.VMEM((n, 2 * n), F32),
            pltpu.VMEM((4, 2, 4, 2 * width, cols // 8), BF16),
            pltpu.VMEM((4, 2, 3, 2 * width, cols // 8), BF16),
            pltpu.VMEM((4, 2, 4, 2 * width, cols // 8), BF16),
            dma((8,)),
            dma((7,)),
            dma((7,)),
            dma((7,)),
            dma((7,)),
            dma((72,)),
            dma((72,)),
        ],
        compiler_params=pltpu.CompilerParams(collective_id=0, has_side_effects=True, vmem_limit_bytes=24 * 2**20),
    )(
        *(
            pltpu.with_memory_space_constraint(a, pltpu.HBM)
            for a in (tile_list, panel.T, trailing.reshape(tiles, TILE, cols))
        )
    )
    return call_finish(tile_list, t, p, cr, u, m)


def solution(mesh):
    return jax.shard_map(
        local,
        mesh=mesh,
        in_specs=(P("row", "col"), P("row", "col"), P("row")),
        out_specs=(P(), P("col", None), P("row", "col")),
        check_vma=False,
    )
```

```python
import functools

import jax
import jax.numpy as jnp
from jax import lax
from jax.experimental import pallas as pl
from jax.experimental.pallas import tpu as pltpu
from jax.sharding import PartitionSpec as P

TILE = 128
MESH = pl.DeviceIdType.MESH
F32 = jnp.float32
BF16 = jnp.bfloat16


def dot(a, b, dims, precision=None):
    return lax.dot_general(a, b, (dims, ((), ())), precision=precision, preferred_element_type=F32)


def spread_entries(d, p):
    a, low, inv = {}, {}, {}
    for i in range(p):
        for j in range(i + 1):
            a[i, j] = jnp.broadcast_to(d[j : j + 1, i : i + 1], (8, 128))
    for j in range(p):
        inv[j, j] = lax.rsqrt(a[j, j])
        for i in range(j, p):
            low[i, j] = a[i, j] * inv[j, j]
        for k in range(j + 1, p):
            for i in range(k, p):
                a[i, k] = a[i, k] - low[i, j] * low[k, j]
    for i in range(p):
        for j in range(i):
            total = sum(low[i, k] * inv[k, j] for k in range(j, i))
            inv[i, j] = -total * inv[i, i]
    return inv


def factor(a_ref, u_ref, m_ref, n, block, p=8):
    lane = 128
    count = 2 * n // lane
    rows = lax.broadcasted_iota(jnp.int32, (8, lane), 0)

    for lo in range(0, n, block):
        groups = [[a_ref[lo + i : lo + i + p, w * lane : (w + 1) * lane] for w in range(count)] for i in range(0, block, p)]
        done = []
        for g in range(block // p):
            at = lo + g * p
            own, off = at // lane, at % lane
            live = [w for w in range(count) if (w >= own if w < count // 2 else w - count // 2 <= own)]
            inv = spread_entries(groups[g][own][:, off : off + p], p)
            columns = []
            for j in range(p):
                column = jnp.zeros((8, lane), F32)
                for i in range(j, p):
                    column = jnp.where(rows == i, inv[i, j], column)
                columns.append(column)
            u = [jnp.zeros((p, lane), F32)] * count
            for w in live:
                u[w] = sum(columns[j] * groups[g][w][j : j + 1, :] for j in range(p))
            done.append(jnp.concatenate(u, axis=1))
            for h in range(g + 1, block // p):
                left = [jnp.broadcast_to(groups[h][own][:, off + q : off + q + 1], (8, lane)) for q in range(p)]
                lower = [sum(left[q] * inv[j, q] for q in range(j + 1)) for j in range(p)]
                for w in live:
                    rest = groups[h][w]
                    for j in range(p):
                        rest = rest - lower[j] * u[w][j : j + 1, :]
                    groups[h][w] = rest
            yield
        full = jnp.concatenate(done, axis=0)
        keep = lax.broadcasted_iota(jnp.int32, (block, n), 1) >= lax.broadcasted_iota(jnp.int32, (block, n), 0) + lo
        u_ref[lo : lo + block, :] = jnp.where(keep, full[:, :n], 0.0)
        m_ref[lo : lo + block, :] = full[:, n:]
        first = lo + block
        if first < n:
            cols = slice(first // lane * lane, n + ((first - 1) // lane + 1) * lane)
            high = full.astype(BF16)
            rest = (full - high.astype(F32)).astype(BF16)
            right = jnp.concatenate([high[:, cols], rest[:, cols], high[:, cols]], axis=0)
            spans = [(first, first + block), (first + block, n)] if first + block < n else [(first, n)]
            for a, b in spans:
                left = jnp.concatenate([high[:, a:b], high[:, a:b], rest[:, a:b]], axis=0)
                a_ref[a:b, cols] -= dot(left, right, ((0,), (0,)))


def fetch_and_reduce(
    tl_hbm, pt_hbm, t_hbm,
    t_out, p_out, cr_out, u_out, m_out,
    tl_ref, pt_ref, pt_out, wide, gx, gy, gz, aug, s1, l1, s2,
    t_sem, p_send, p_recv, g_send, g_recv, c_send, c_recv,
):
    width, active = pt_ref.shape[0], tl_ref.shape[0]
    n = 8 * width
    pair = 2 * width
    tiles = t_out.shape[0]
    spare = tiles - active
    part = t_out.shape[2] // 8
    r, c = lax.axis_index("row"), lax.axis_index("col")
    x, y, z, k = r // 4, lax.rem(r, 4), c // 2, lax.rem(c, 2)

    def along_x(d):
        return (lax.rem(x + d, 4) * 4 + y, c)

    def along_y(d):
        return (x * 4 + lax.rem(y + d, 4), c)

    def along_z(d):
        return (r, lax.rem(z + d, 4) * 2 + k)

    sibling = (r, z * 2 + 1 - k)

    barrier = pltpu.get_barrier_semaphore()
    partners = [f(d) for f in (along_x, along_y, along_z) for d in (1, 2, 3)] + [sibling]
    for partner in partners:
        pl.semaphore_signal(barrier, inc=1, device_id=partner, device_id_type=MESH)

    early = [pltpu.make_async_copy(tl_hbm, tl_ref, t_sem.at[6]), pltpu.make_async_copy(pt_hbm, pt_ref, t_sem.at[7])]
    for copy in early:
        copy.start()
    loads = []
    for i in range(6):
        copy = pltpu.make_async_copy(t_hbm.at[pl.ds(4 * i, 4)], t_out.at[pl.ds(4 * i, 4)], t_sem.at[i])
        copy.start()
        loads.append(copy)

    for copy in early:
        copy.wait()
    for j in range(active):
        pick = pt_ref[:, (j + spare) * TILE : (j + spare + 1) * TILE]
        for i in reversed(range(spare)):
            pick = jnp.where(tl_ref[j] == j + i, pt_ref[:, (j + i) * TILE : (j + i + 1) * TILE], pick)
        pt_out[z, k, :, j * TILE : (j + 1) * TILE] = pick
    pl.semaphore_wait(barrier, len(partners))

    def send(src, dst, send_sem, recv_sem, to):
        copy = pltpu.make_async_remote_copy(
            src_ref=src, dst_ref=dst, send_sem=send_sem, recv_sem=recv_sem, device_id=to, device_id_type=MESH
        )
        copy.start()
        return copy

    def finish_all(copies):
        for copy in copies:
            copy.wait()

    own = pt_out.at[z, k]
    near = send(own, own, p_send.at[0], p_recv.at[0], sibling)
    far = {d: send(own, own, p_send.at[d], p_recv.at[d], along_z(d)) for d in (1, 3, 2)}

    def source(d):
        return lax.rem(z + 4 - d, 4)

    def relay(d):
        far[d].wait_recv()
        block = pt_out.at[source(d), k]
        return send(block, block, p_send.at[3 + d], p_recv.at[3 + d], sibling)

    def lanes(h):
        return (along_x, along_y, x, y) if h == 0 else (along_y, along_x, y, x)

    def cross(chunks):
        for d in chunks:
            for j in range(tiles):
                spread = jnp.zeros((2, width, TILE), BF16)
                for i in range(max(j - spare, 0), min(j, active - 1) + 1):
                    spread = jnp.where(tl_ref[i] == j, pt_out[source(d), :, :, i * TILE : (i + 1) * TILE], spread)
                wide[d, :, j * TILE : (j + 1) * TILE] = spread.reshape(pair, TILE)
        lhs = jnp.concatenate([wide[d] for d in chunks], axis=0)
        for h in range(2):
            for t in range(2):
                at = (2 * h + t) * 2 * part
                rhs = t_out[:, :, at : at + 2 * part].reshape(tiles * TILE, 2 * part)
                product = dot(lhs, rhs, ((1,), (0,))).astype(BF16)
                for i, d in enumerate(chunks):
                    s1[d, h, 2 * t] = product[i * pair : (i + 1) * pair, :part]
                    s1[d, h, 2 * t + 1] = product[i * pair : (i + 1) * pair, part:]
            a, _, ma, _ = lanes(h)
            for d in chunks:
                sem = 9 * (2 * d + h) - 1
                stage1[d, h] = [
                    send(s1.at[d, h, lax.rem(ma + e, 4)], l1.at[d, h, e - 1], c_send.at[sem + e], c_recv.at[sem + e], a(e))
                    for e in (2, 1, 3)
                ]

    def second(d):
        for h in range(2):
            _, b, ma, mb = lanes(h)
            finish_all(stage1[d, h])
            total = s1[d, h, ma].astype(F32)
            for e in range(3):
                total = total + l1[d, h, e].astype(F32)
            block = s2.at[d, h, mb]
            block[...] = total.astype(BF16)
            sem = 9 * (2 * d + h) + 2
            stage2[d, h] = [send(block, block, c_send.at[sem + e], c_recv.at[sem + e], b(e)) for e in (2, 1, 3)]

    def third(d):
        for h in range(2):
            a, _, ma, _ = lanes(h)
            finish_all(stage2[d, h])
            total = s2[d, h, 0].astype(F32)
            for e in range(1, 4):
                total = total + s2[d, h, e].astype(F32)
            block = cr_out.at[source(d), h, ma]
            block[...] = total.astype(BF16)
            sem = 9 * (2 * d + h) + 5
            stage3.extend(send(block, block, c_send.at[sem + e], c_recv.at[sem + e], a(e)) for e in (2, 1, 3))

    eye = lax.broadcasted_iota(jnp.int32, (n, n), 0) == lax.broadcasted_iota(jnp.int32, (n, n), 1)
    aug[:, n:] = jnp.where(eye, 1.0, 0.0)
    stage1, stage2, stage3 = {}, {}, []
    near.wait_recv()
    finish_all(loads)
    cross((0,))
    relays = [relay(1), relay(3)]
    for copy in relays:
        copy.wait_recv()
    cross((1, 3))
    second(0)
    relays.append(relay(2))
    relays[2].wait_recv()

    everything = pt_out[...].reshape(n, active * TILE)
    half = pt_out[pl.ds(2 * k, 2)].reshape(n // 2, active * TILE)
    gx[x] = dot(half, everything, ((1,), (1,))).astype(BF16)
    over_x = [send(gx.at[x], gx.at[x], g_send.at[e - 1], g_recv.at[e - 1], along_x(e)) for e in (2, 1, 3)]
    cross((2,))

    for i in range(0, active * TILE, 2 * TILE):
        p_out[i : i + 2 * TILE, :] = pt_out[:, :, :, i : i + 2 * TILE].reshape(n, 2 * TILE).T
    finish_all(over_x)
    gy[y] = (gx[0].astype(F32) + gx[1].astype(F32) + gx[2].astype(F32) + gx[3].astype(F32)).astype(BF16)
    over_y = [send(gy.at[y], gy.at[y], g_send.at[2 + e], g_recv.at[2 + e], along_y(e)) for e in (2, 1, 3)]
    second(1)
    second(3)
    second(2)
    finish_all(over_y)
    gz[k] = gy[0].astype(F32) + gy[1].astype(F32) + gy[2].astype(F32) + gy[3].astype(F32)
    swap = send(gz.at[k], gz.at[k], g_send.at[6], g_recv.at[6], sibling)
    third(0)
    swap.wait()
    aug[:, :n] = gz[...].reshape(n, n)
    steps = factor(aug, u_out, m_out, n, 32)
    for _ in range(3):
        next(steps)
    third(1)
    third(3)
    for _ in range(6):
        next(steps)
    third(2)
    for _ in steps:
        pass
    finish_all(stage3)
    near.wait_send()
    for copy in relays:
        copy.wait_send()
    for copy in far.values():
        copy.wait_send()


def finish(tl_ref, t_ref, p_ref, cr_ref, u_ref, m_ref, tri_ref, top_hbm, up_hbm, tops, outs, top_sem, out_sem):
    n = m_ref.shape[0]
    active = tl_ref.shape[0]
    part = t_ref.shape[2] // 4
    tri_ref[...] = u_ref[...]
    m = m_ref[...]
    mh = m.astype(BF16)
    ml = (m - mh.astype(F32)).astype(BF16)
    copies = []
    for q in range(4):
        cols = slice(q * part, (q + 1) * part)
        blocks = [cr_ref[:, q // 2, 2 * (q % 2) + e].reshape(n, part // 2) for e in range(2)]
        cross = jnp.concatenate(blocks, axis=1)
        top = dot(mh, cross, ((1,), (0,))) + dot(ml, cross, ((1,), (0,)))
        coeff = dot(mh, top.astype(BF16), ((0,), (0,))).astype(BF16)
        tops[q] = top.T
        copy = pltpu.make_async_copy(tops.at[q], top_hbm.at[pl.ds(q * part, part)], top_sem.at[q])
        copy.start()
        copies.append(copy)
        for i in range(active // 2):
            rows = slice(2 * i * TILE, 2 * (i + 1) * TILE)
            product = dot(p_ref[rows, :], coeff, ((1,), (0,)))
            old = jnp.concatenate([t_ref[tl_ref[2 * i + e], :, cols] for e in range(2)], axis=0)
            outs[rows, cols] = (old.astype(F32) - product).astype(BF16)
            copy = pltpu.make_async_copy(outs.at[rows, cols], up_hbm.at[rows, cols], out_sem.at[q, i])
            copy.start()
            copies.append(copy)
    for copy in copies:
        copy.wait()


def call_finish(tile_list, t, p, cr, u, m):
    vmem = pl.BlockSpec(memory_space=pltpu.VMEM)
    smem = pl.BlockSpec(memory_space=pltpu.SMEM)
    anywhere = pl.BlockSpec(memory_space=pl.ANY)
    n = m.shape[0]
    cols = t.shape[2]
    active = tile_list.shape[0]
    return pl.pallas_call(
        finish,
        out_shape=(
            jax.ShapeDtypeStruct((n, n), F32),
            jax.ShapeDtypeStruct((cols, n), F32),
            jax.ShapeDtypeStruct((active * TILE, cols), BF16),
        ),
        in_specs=[smem] + [vmem] * 5,
        out_specs=[vmem, anywhere, anywhere],
        scratch_shapes=[
            pltpu.VMEM((4, cols // 4, n), F32),
            pltpu.VMEM((active * TILE, cols), BF16),
            pltpu.SemaphoreType.DMA((4,)),
            pltpu.SemaphoreType.DMA((4, active // 2)),
        ],
        compiler_params=pltpu.CompilerParams(vmem_limit_bytes=24 * 2**20),
    )(tile_list, t, p, cr, u, m)


def local(panel, trailing, tile_list):
    rows, width = panel.shape
    cols = trailing.shape[1]
    active = tile_list.shape[0]
    tiles = rows // TILE
    n = 8 * width
    vmem = pl.BlockSpec(memory_space=pltpu.VMEM)
    hbm = pl.BlockSpec(memory_space=pltpu.HBM)
    dma = pltpu.SemaphoreType.DMA
    t, p, cr, u, m = pl.pallas_call(
        fetch_and_reduce,
        out_shape=(
            pltpu.VMEM((tiles, TILE, cols), BF16),
            pltpu.VMEM((active * TILE, n), BF16),
            pltpu.VMEM((4, 2, 4, 2 * width, cols // 8), BF16),
            pltpu.VMEM((n, n), F32),
            pltpu.VMEM((n, n), F32),
        ),
        in_specs=[hbm] * 3,
        out_specs=[vmem] * 5,
        scratch_shapes=[
            pltpu.SMEM((active,), jnp.int32),
            pltpu.VMEM((width, rows), BF16),
            pltpu.VMEM((4, 2, width, active * TILE), BF16),
            pltpu.VMEM((4, 2 * width, rows), BF16),
            pltpu.VMEM((4, n // 2, n), BF16),
            pltpu.VMEM((4, n // 2, n), BF16),
            pltpu.VMEM((2, n // 2, n), F32),
            pltpu.VMEM((n, 2 * n), F32),
            pltpu.VMEM((4, 2, 4, 2 * width, cols // 8), BF16),
            pltpu.VMEM((4, 2, 3, 2 * width, cols // 8), BF16),
            pltpu.VMEM((4, 2, 4, 2 * width, cols // 8), BF16),
            dma((8,)),
            dma((7,)),
            dma((7,)),
            dma((7,)),
            dma((7,)),
            dma((72,)),
            dma((72,)),
        ],
        compiler_params=pltpu.CompilerParams(collective_id=0, has_side_effects=True, vmem_limit_bytes=24 * 2**20),
    )(
        *(
            pltpu.with_memory_space_constraint(a, pltpu.HBM)
            for a in (tile_list, panel.T, trailing.reshape(tiles, TILE, cols))
        )
    )
    return call_finish(tile_list, t, p, cr, u, m)


def solution(mesh):
    return jax.shard_map(
        local,
        mesh=mesh,
        in_specs=(P("row", "col"), P("row", "col"), P("row")),
        out_specs=(P(), P("col", None), P("row", "col")),
        check_vma=False,
    )
```

```python
import functools

import jax
import jax.numpy as jnp
from jax import lax
from jax.experimental import pallas as pl
from jax.experimental.pallas import tpu as pltpu
from jax.sharding import PartitionSpec as P

TILE = 128
MESH = pl.DeviceIdType.MESH
F32 = jnp.float32
BF16 = jnp.bfloat16


def dot(a, b, dims, precision=None):
    return lax.dot_general(a, b, (dims, ((), ())), precision=precision, preferred_element_type=F32)


def spread_entries(d, p):
    a, low, inv = {}, {}, {}
    for i in range(p):
        for j in range(i + 1):
            a[i, j] = jnp.broadcast_to(d[j : j + 1, i : i + 1], (8, 128))
    for j in range(p):
        inv[j, j] = lax.rsqrt(a[j, j])
        for i in range(j, p):
            low[i, j] = a[i, j] * inv[j, j]
        for k in range(j + 1, p):
            for i in range(k, p):
                a[i, k] = a[i, k] - low[i, j] * low[k, j]
    for i in range(p):
        for j in range(i):
            total = sum(low[i, k] * inv[k, j] for k in range(j, i))
            inv[i, j] = -total * inv[i, i]
    return inv


def factor(a_ref, u_ref, m_ref, n, block, p=8):
    lane = 128
    count = 2 * n // lane
    rows = lax.broadcasted_iota(jnp.int32, (8, lane), 0)

    for lo in range(0, n, block):
        groups = [[a_ref[lo + i : lo + i + p, w * lane : (w + 1) * lane] for w in range(count)] for i in range(0, block, p)]
        done = []
        for g in range(block // p):
            at = lo + g * p
            own, off = at // lane, at % lane
            live = [w for w in range(count) if (w >= own if w < count // 2 else w - count // 2 <= own)]
            inv = spread_entries(groups[g][own][:, off : off + p], p)
            columns = []
            for j in range(p):
                column = jnp.zeros((8, lane), F32)
                for i in range(j, p):
                    column = jnp.where(rows == i, inv[i, j], column)
                columns.append(column)
            u = [jnp.zeros((p, lane), F32)] * count
            for w in live:
                u[w] = sum(columns[j] * groups[g][w][j : j + 1, :] for j in range(p))
            done.append(jnp.concatenate(u, axis=1))
            for h in range(g + 1, block // p):
                left = [jnp.broadcast_to(groups[h][own][:, off + q : off + q + 1], (8, lane)) for q in range(p)]
                lower = [sum(left[q] * inv[j, q] for q in range(j + 1)) for j in range(p)]
                for w in live:
                    rest = groups[h][w]
                    for j in range(p):
                        rest = rest - lower[j] * u[w][j : j + 1, :]
                    groups[h][w] = rest
            yield
        full = jnp.concatenate(done, axis=0)
        keep = lax.broadcasted_iota(jnp.int32, (block, n), 1) >= lax.broadcasted_iota(jnp.int32, (block, n), 0) + lo
        u_ref[lo : lo + block, :] = jnp.where(keep, full[:, :n], 0.0)
        m_ref[lo : lo + block, :] = full[:, n:]
        first = lo + block
        if first < n:
            cols = slice(first // lane * lane, n + ((first - 1) // lane + 1) * lane)
            high = full.astype(BF16)
            rest = (full - high.astype(F32)).astype(BF16)
            right = jnp.concatenate([high[:, cols], rest[:, cols], high[:, cols]], axis=0)
            spans = [(first, first + block), (first + block, n)] if first + block < n else [(first, n)]
            for a, b in spans:
                left = jnp.concatenate([high[:, a:b], high[:, a:b], rest[:, a:b]], axis=0)
                a_ref[a:b, cols] -= dot(left, right, ((0,), (0,)))


def fetch_and_reduce(
    tl_hbm, pt_hbm, t_hbm,
    t_out, p_out, cr_out, u_out, m_out,
    tl_ref, pt_ref, pt_out, wide, gx, gy, gz, aug, s1, l1, s2,
    t_sem, p_send, p_recv, g_send, g_recv, c_send, c_recv,
):
    width, active = pt_ref.shape[0], tl_ref.shape[0]
    n = 8 * width
    pair = 2 * width
    tiles = t_out.shape[0]
    spare = tiles - active
    part = t_out.shape[2] // 8
    r, c = lax.axis_index("row"), lax.axis_index("col")
    x, y, z, k = r // 4, lax.rem(r, 4), c // 2, lax.rem(c, 2)

    def along_x(d):
        return (lax.rem(x + d, 4) * 4 + y, c)

    def along_y(d):
        return (x * 4 + lax.rem(y + d, 4), c)

    def along_z(d):
        return (r, lax.rem(z + d, 4) * 2 + k)

    sibling = (r, z * 2 + 1 - k)

    barrier = pltpu.get_barrier_semaphore()
    partners = [f(d) for f in (along_x, along_y, along_z) for d in (1, 2, 3)] + [sibling]
    for partner in partners:
        pl.semaphore_signal(barrier, inc=1, device_id=partner, device_id_type=MESH)

    early = [pltpu.make_async_copy(tl_hbm, tl_ref, t_sem.at[6]), pltpu.make_async_copy(pt_hbm, pt_ref, t_sem.at[7])]
    for copy in early:
        copy.start()
    loads = []
    for i in range(6):
        copy = pltpu.make_async_copy(t_hbm.at[pl.ds(4 * i, 4)], t_out.at[pl.ds(4 * i, 4)], t_sem.at[i])
        copy.start()
        loads.append(copy)

    for copy in early:
        copy.wait()
    for j in range(active):
        pick = pt_ref[:, (j + spare) * TILE : (j + spare + 1) * TILE]
        for i in reversed(range(spare)):
            pick = jnp.where(tl_ref[j] == j + i, pt_ref[:, (j + i) * TILE : (j + i + 1) * TILE], pick)
        pt_out[z, k, :, j * TILE : (j + 1) * TILE] = pick
    pl.semaphore_wait(barrier, len(partners))

    def send(src, dst, send_sem, recv_sem, to):
        copy = pltpu.make_async_remote_copy(
            src_ref=src, dst_ref=dst, send_sem=send_sem, recv_sem=recv_sem, device_id=to, device_id_type=MESH
        )
        copy.start()
        return copy

    def finish_all(copies):
        for copy in copies:
            copy.wait()

    own = pt_out.at[z, k]
    near = send(own, own, p_send.at[0], p_recv.at[0], sibling)
    far = {d: send(own, own, p_send.at[d], p_recv.at[d], along_z(d)) for d in (1, 3, 2)}

    def source(d):
        return lax.rem(z + 4 - d, 4)

    def relay(d):
        far[d].wait_recv()
        block = pt_out.at[source(d), k]
        return send(block, block, p_send.at[3 + d], p_recv.at[3 + d], sibling)

    def lanes(h):
        return (along_x, along_y, x, y) if h == 0 else (along_y, along_x, y, x)

    def cross(chunks):
        for d in chunks:
            for j in range(tiles):
                spread = jnp.zeros((2, width, TILE), BF16)
                for i in range(max(j - spare, 0), min(j, active - 1) + 1):
                    spread = jnp.where(tl_ref[i] == j, pt_out[source(d), :, :, i * TILE : (i + 1) * TILE], spread)
                wide[d, :, j * TILE : (j + 1) * TILE] = spread.reshape(pair, TILE)
        lhs = jnp.concatenate([wide[d] for d in chunks], axis=0)
        for h in range(2):
            for t in range(2):
                at = (2 * h + t) * 2 * part
                rhs = t_out[:, :, at : at + 2 * part].reshape(tiles * TILE, 2 * part)
                product = dot(lhs, rhs, ((1,), (0,))).astype(BF16)
                for i, d in enumerate(chunks):
                    s1[d, h, 2 * t] = product[i * pair : (i + 1) * pair, :part]
                    s1[d, h, 2 * t + 1] = product[i * pair : (i + 1) * pair, part:]
            a, _, ma, _ = lanes(h)
            for d in chunks:
                sem = 9 * (2 * d + h) - 1
                stage1[d, h] = [
                    send(s1.at[d, h, lax.rem(ma + e, 4)], l1.at[d, h, e - 1], c_send.at[sem + e], c_recv.at[sem + e], a(e))
                    for e in (2, 1, 3)
                ]

    def second(d):
        for h in range(2):
            _, b, ma, mb = lanes(h)
            finish_all(stage1[d, h])
            total = s1[d, h, ma].astype(F32)
            for e in range(3):
                total = total + l1[d, h, e].astype(F32)
            block = s2.at[d, h, mb]
            block[...] = total.astype(BF16)
            sem = 9 * (2 * d + h) + 2
            stage2[d, h] = [send(block, block, c_send.at[sem + e], c_recv.at[sem + e], b(e)) for e in (2, 1, 3)]

    def third(d):
        for h in range(2):
            a, _, ma, _ = lanes(h)
            finish_all(stage2[d, h])
            total = s2[d, h, 0].astype(F32)
            for e in range(1, 4):
                total = total + s2[d, h, e].astype(F32)
            block = cr_out.at[source(d), h, ma]
            block[...] = total.astype(BF16)
            sem = 9 * (2 * d + h) + 5
            stage3.extend(send(block, block, c_send.at[sem + e], c_recv.at[sem + e], a(e)) for e in (2, 1, 3))

    eye = lax.broadcasted_iota(jnp.int32, (n, n), 0) == lax.broadcasted_iota(jnp.int32, (n, n), 1)
    aug[:, n:] = jnp.where(eye, 1.0, 0.0)
    stage1, stage2, stage3 = {}, {}, []
    near.wait_recv()
    finish_all(loads)
    cross((0,))
    relays = [relay(1), relay(3)]
    for copy in relays:
        copy.wait_recv()
    cross((1, 3))
    relays.append(relay(2))
    second(0)
    relays[2].wait_recv()

    everything = pt_out[...].reshape(n, active * TILE)
    half = pt_out[pl.ds(2 * k, 2)].reshape(n // 2, active * TILE)
    gx[x] = dot(half, everything, ((1,), (1,))).astype(BF16)
    over_x = [send(gx.at[x], gx.at[x], g_send.at[e - 1], g_recv.at[e - 1], along_x(e)) for e in (2, 1, 3)]
    cross((2,))

    for i in range(0, active * TILE, 2 * TILE):
        p_out[i : i + 2 * TILE, :] = pt_out[:, :, :, i : i + 2 * TILE].reshape(n, 2 * TILE).T
    finish_all(over_x)
    gy[y] = (gx[0].astype(F32) + gx[1].astype(F32) + gx[2].astype(F32) + gx[3].astype(F32)).astype(BF16)
    over_y = [send(gy.at[y], gy.at[y], g_send.at[2 + e], g_recv.at[2 + e], along_y(e)) for e in (2, 1, 3)]
    second(1)
    second(3)
    second(2)
    finish_all(over_y)
    gz[k] = gy[0].astype(F32) + gy[1].astype(F32) + gy[2].astype(F32) + gy[3].astype(F32)
    swap = send(gz.at[k], gz.at[k], g_send.at[6], g_recv.at[6], sibling)
    third(0)
    swap.wait()
    aug[:, :n] = gz[...].reshape(n, n)
    steps = factor(aug, u_out, m_out, n, 32)
    for _ in range(3):
        next(steps)
    third(1)
    third(3)
    for _ in range(6):
        next(steps)
    third(2)
    for _ in steps:
        pass
    finish_all(stage3)
    near.wait_send()
    for copy in relays:
        copy.wait_send()
    for copy in far.values():
        copy.wait_send()


def finish(tl_ref, t_ref, p_ref, cr_ref, u_ref, m_ref, tri_ref, top_hbm, up_hbm, tops, outs, top_sem, out_sem):
    n = m_ref.shape[0]
    active = tl_ref.shape[0]
    part = t_ref.shape[2] // 4
    tri_ref[...] = u_ref[...]
    m = m_ref[...]
    mh = m.astype(BF16)
    ml = (m - mh.astype(F32)).astype(BF16)
    copies = []
    for q in range(4):
        cols = slice(q * part, (q + 1) * part)
        blocks = [cr_ref[:, q // 2, 2 * (q % 2) + e].reshape(n, part // 2) for e in range(2)]
        cross = jnp.concatenate(blocks, axis=1)
        top = dot(mh, cross, ((1,), (0,))) + dot(ml, cross, ((1,), (0,)))
        coeff = dot(mh, top.astype(BF16), ((0,), (0,))).astype(BF16)
        tops[q] = top.T
        copy = pltpu.make_async_copy(tops.at[q], top_hbm.at[pl.ds(q * part, part)], top_sem.at[q])
        copy.start()
        copies.append(copy)
        for i in range(active // 2):
            rows = slice(2 * i * TILE, 2 * (i + 1) * TILE)
            product = dot(p_ref[rows, :], coeff, ((1,), (0,)))
            old = jnp.concatenate([t_ref[tl_ref[2 * i + e], :, cols] for e in range(2)], axis=0)
            outs[rows, cols] = (old.astype(F32) - product).astype(BF16)
            copy = pltpu.make_async_copy(outs.at[rows, cols], up_hbm.at[rows, cols], out_sem.at[q, i])
            copy.start()
            copies.append(copy)
    for copy in copies:
        copy.wait()


def call_finish(tile_list, t, p, cr, u, m):
    vmem = pl.BlockSpec(memory_space=pltpu.VMEM)
    smem = pl.BlockSpec(memory_space=pltpu.SMEM)
    anywhere = pl.BlockSpec(memory_space=pl.ANY)
    n = m.shape[0]
    cols = t.shape[2]
    active = tile_list.shape[0]
    return pl.pallas_call(
        finish,
        out_shape=(
            jax.ShapeDtypeStruct((n, n), F32),
            jax.ShapeDtypeStruct((cols, n), F32),
            jax.ShapeDtypeStruct((active * TILE, cols), BF16),
        ),
        in_specs=[smem] + [vmem] * 5,
        out_specs=[vmem, anywhere, anywhere],
        scratch_shapes=[
            pltpu.VMEM((4, cols // 4, n), F32),
            pltpu.VMEM((active * TILE, cols), BF16),
            pltpu.SemaphoreType.DMA((4,)),
            pltpu.SemaphoreType.DMA((4, active // 2)),
        ],
        compiler_params=pltpu.CompilerParams(vmem_limit_bytes=24 * 2**20),
    )(tile_list, t, p, cr, u, m)


def local(panel, trailing, tile_list):
    rows, width = panel.shape
    cols = trailing.shape[1]
    active = tile_list.shape[0]
    tiles = rows // TILE
    n = 8 * width
    vmem = pl.BlockSpec(memory_space=pltpu.VMEM)
    hbm = pl.BlockSpec(memory_space=pltpu.HBM)
    dma = pltpu.SemaphoreType.DMA
    t, p, cr, u, m = pl.pallas_call(
        fetch_and_reduce,
        out_shape=(
            pltpu.VMEM((tiles, TILE, cols), BF16),
            pltpu.VMEM((active * TILE, n), BF16),
            pltpu.VMEM((4, 2, 4, 2 * width, cols // 8), BF16),
            pltpu.VMEM((n, n), F32),
            pltpu.VMEM((n, n), F32),
        ),
        in_specs=[hbm] * 3,
        out_specs=[vmem] * 5,
        scratch_shapes=[
            pltpu.SMEM((active,), jnp.int32),
            pltpu.VMEM((width, rows), BF16),
            pltpu.VMEM((4, 2, width, active * TILE), BF16),
            pltpu.VMEM((4, 2 * width, rows), BF16),
            pltpu.VMEM((4, n // 2, n), BF16),
            pltpu.VMEM((4, n // 2, n), BF16),
            pltpu.VMEM((2, n // 2, n), F32),
            pltpu.VMEM((n, 2 * n), F32),
            pltpu.VMEM((4, 2, 4, 2 * width, cols // 8), BF16),
            pltpu.VMEM((4, 2, 3, 2 * width, cols // 8), BF16),
            pltpu.VMEM((4, 2, 4, 2 * width, cols // 8), BF16),
            dma((8,)),
            dma((7,)),
            dma((7,)),
            dma((7,)),
            dma((7,)),
            dma((72,)),
            dma((72,)),
        ],
        compiler_params=pltpu.CompilerParams(collective_id=0, has_side_effects=True, vmem_limit_bytes=24 * 2**20),
    )(
        *(
            pltpu.with_memory_space_constraint(a, pltpu.HBM)
            for a in (tile_list, panel.T, trailing.reshape(tiles, TILE, cols))
        )
    )
    return call_finish(tile_list, t, p, cr, u, m)


def solution(mesh):
    return jax.shard_map(
        local,
        mesh=mesh,
        in_specs=(P("row", "col"), P("row", "col"), P("row")),
        out_specs=(P(), P("col", None), P("row", "col")),
        check_vma=False,
    )
```
